32 devices in a mesh: dp: 4 (over y, x), seq: 8 (over z, core).
Axes of the slice: x: 2, y: 2, z: 4, core: 2. Of those that a mesh axis runs over, the one named last changes fastest.
Arguments:
- query: float32 [4, 256, 1024], P('dp', None, 'seq'), may hold values from -6 to 6
- key_in: float32 [4, 256, 1024], P('dp', None, 'seq'), may hold values from -6 to 6
- value: float32 [4, 256, 1024], P('dp', None, 'seq'), may hold values from -6 to 6
- grad_out: float32 [4, 256, 1024], P('dp', None, 'seq'), may hold values from -6 to 6
- filt: float32 [256, 1024], P('seq'), may hold values from -0.1875 to 0.1875
Outputs:
- output: float32 [4, 256, 1024], P('dp', None, 'seq')
- grad_query: float32 [4, 256, 1024], P('dp', None, 'seq')
- grad_key: float32 [4, 256, 1024], P('dp', None, 'seq')
- grad_value: float32 [4, 256, 1024], P('dp', None, 'seq')
- grad_filt: float32 [256, 1024], P('seq')
The draws below stay inside these ranges and needn't reach their ends.
All inputs are finite; a program needn't handle non-finite values.
Results may differ from the reference program's by a relative error of at most 0.00016.
Values sent between devices are 32-bit elements; how exact they have to be, the bound alone decides.
A program may use at most 64 MiB of HBM per device.

```python
import math
import jax
import jax.numpy as jnp
from jax import lax

C = 256
LENGTH = 1024
BATCH = 4
PADDED = 2048


def block_scale(stream_key, shape, pieces, low, high):
    def one(axis_at, shards_of):
        heights = jax.random.uniform(jax.random.fold_in(jax.random.fold_in(stream_key, 6), axis_at), (shards_of,), jnp.float32, low / len(pieces), high / len(pieces))
        return jnp.repeat(jnp.exp(heights), shape[axis_at] // shards_of).reshape((-1,) + (1,) * (len(shape) - axis_at - 1))

    gain = one(*pieces[0])
    for cut in pieces[1:]:
        gain = gain * one(*cut)
    return gain


def normal_values(key, extent, deviation, bound, cuts=(), kind=jnp.bfloat16):
    drawn = jax.random.normal(key, extent, jnp.float32) * deviation
    if len(cuts) > 0:
        drawn = block_scale(key, extent, cuts, -0.22, 0.18) * drawn
    return jnp.clip(drawn, min=-bound, max=bound).astype(kind)


def setup_inputs(seed: int = 0) -> dict:
    key_of = jax.random.split(jax.random.key(seed), 6)
    query = normal_values(key_of[0], (BATCH, C, LENGTH), 1.0, 6.0, ((0, 4), (2, 8)), jnp.float32)
    key_in = normal_values(key_of[1], (BATCH, C, LENGTH), 1.0, 6.0, ((0, 4), (2, 8)), jnp.float32)
    value = normal_values(key_of[2], (BATCH, C, LENGTH), 1.0, 6.0, ((0, 4), (2, 8)), jnp.float32)
    grad_out = normal_values(key_of[3], (BATCH, C, LENGTH), 1.0, 6.0, ((0, 4), (2, 8)), jnp.float32)
    filt = normal_values(key_of[4], (C, LENGTH), LENGTH ** -0.5, 0.1875, ((0, 8),), jnp.float32)
    return dict(query=query, key_in=key_in, value=value, grad_out=grad_out, filt=filt)


def one_sequence(items, filt_spec):
    query, key_in, value, grad_out = items
    gated = key_in * value
    grad_conv = grad_out * query
    gated_spec = jnp.fft.rfft(gated, n=PADDED, axis=-1)
    grad_spec = jnp.fft.rfft(grad_conv, n=PADDED, axis=-1)
    conv = jnp.fft.irfft(filt_spec * gated_spec, n=PADDED, axis=-1)[:, :LENGTH]
    grad_gated = jnp.fft.irfft(jnp.conj(filt_spec) * grad_spec, n=PADDED, axis=-1)[:, :LENGTH]
    filt_part = jnp.fft.irfft(jnp.conj(gated_spec) * grad_spec, n=PADDED, axis=-1)[:, :LENGTH]
    return (query * conv, grad_out * conv, grad_gated * value, grad_gated * key_in, filt_part)

def reference(query, key_in, value, grad_out, filt):
    filt_spec = jnp.fft.rfft(filt, n=PADDED, axis=-1)
    output, grad_query, grad_key, grad_value, filt_parts = lax.map(lambda items: one_sequence(items, filt_spec), (query, key_in, value, grad_out))
    grad_filt = lax.optimization_barrier(jnp.sum(filt_parts, axis=0)) / math.sqrt(BATCH * LENGTH)
    return (output, grad_query, grad_key, grad_value, grad_filt)
```

```python
import functools
import math

import jax
import jax.numpy as jnp
import ml_dtypes
import numpy as np
from jax import lax
from jax.experimental import pallas as pl
from jax.experimental.pallas import tpu as pltpu
from jax.sharding import PartitionSpec as P

MESH = pl.DeviceIdType.MESH
BLOCK = 128
CHUNK = 8
UNROLL = 8


def tables():
    place = np.arange(BLOCK, dtype=np.float64)
    angle = np.pi * place[:, None] * (2.0 * place[None, :] + 1.0) / (2 * BLOCK)
    ahead = np.concatenate([np.cos(angle), -np.sin(angle)], axis=1)
    back = ahead.T / BLOCK

    def split(table):
        high = table.astype(ml_dtypes.bfloat16)
        low = (table - high.astype(np.float64)).astype(ml_dtypes.bfloat16)
        return (high, low)

    return split(ahead) + split(back)


def dot3(x, high, low):
    x_high = x.astype(jnp.bfloat16)
    x_low = (x - x_high.astype(jnp.float32)).astype(jnp.bfloat16)
    dot = functools.partial(jnp.dot, preferred_element_type=jnp.float32)
    return dot(x_high, high) + (dot(x_low, high) + dot(x_high, low))


def fold(low, high, step, carry):
    if isinstance(low, int) and isinstance(high, int):
        for at in range(low, high):
            carry = step(at, carry)
        return carry
    return lax.fori_loop(low, high, step, carry)


def each(count, step):
    if count <= UNROLL:
        for at in range(count):
            step(at)
    else:

        @pl.loop(0, count)
        def _(at):
            step(at)


def kernel(
    n, nd, ch, cc, scale,
    q_hbm, k_hbm, v_hbm, g_hbm, f_hbm, wh_hbm, wl_hbm, ah_hbm, al_hbm,
    out_q, out_g, out_k, out_v, out_f,
    q, k, v, g, f, wh, wl, ah, al,
    send, recv, fs, xs, hs, zs, ret, back, fb,
    load_sem, s_sem, r_sem, bs_sem, br_sem, fs_sem, fr_sem,
):
    me = lax.axis_index("seq")
    row = lax.axis_index("dp")
    chunks = ch // cc
    offsets = sorted(range(1, n), key=lambda o: -min(o, n - o))

    loads = [
        pltpu.make_async_copy(src, dst, load_sem.at[at])
        for at, (src, dst) in enumerate(
            [
                (k_hbm.at[0], k), (v_hbm.at[0], v), (q_hbm.at[0], q), (g_hbm.at[0], g),
                (f_hbm, f), (wh_hbm, wh), (wl_hbm, wl), (ah_hbm, ah), (al_hbm, al),
            ]
        )
    ]
    for load in loads:
        load.start()

    barrier = pltpu.get_barrier_semaphore()
    for o in range(1, n):
        pl.semaphore_signal(
            barrier, inc=1, device_id={"seq": lax.rem(me + o, n)}, device_id_type=MESH
        )
    for o in range(1, nd):
        pl.semaphore_signal(
            barrier, inc=1, device_id={"dp": lax.rem(row + o, nd)}, device_id_type=MESH
        )

    for load in loads[:4]:
        load.wait()

    def stage(c):
        for p in range(n):
            rows = pl.ds(p * ch + c * cc, cc)
            send[p, c, 0] = k[rows, :] * v[rows, :]
            send[p, c, 1] = g[rows, :] * q[rows, :]
        recv[c, me] = send[me, c]

    def out_copy(c, o):
        to = lax.rem(me + o, n)
        return pltpu.make_async_remote_copy(
            src_ref=send.at[to, c],
            dst_ref=recv.at[c, me],
            send_sem=s_sem.at[c, o - 1],
            recv_sem=r_sem.at[c, o - 1],
            device_id={"seq": to},
            device_id_type=MESH,
        )

    def back_copy(c, o):
        to = lax.rem(me + o, n)
        return pltpu.make_async_remote_copy(
            src_ref=ret.at[c, to],
            dst_ref=back.at[me, c],
            send_sem=bs_sem.at[c, o - 1],
            recv_sem=br_sem.at[c, o - 1],
            device_id={"seq": to},
            device_id_type=MESH,
        )

    def filt_copy(c, o):
        return pltpu.make_async_remote_copy(
            src_ref=fb.at[row, c],
            dst_ref=fb.at[row, c],
            send_sem=fs_sem.at[c, o - 1],
            recv_sem=fr_sem.at[c, o - 1],
            device_id={"dp": lax.rem(row + o, nd)},
            device_id_type=MESH,
        )

    for c in range(chunks):
        stage(c)
        if c == 0:
            pl.semaphore_wait(barrier, n - 1 + nd - 1)
        for o in offsets:
            out_copy(c, o).start()

    for load in loads[4:]:
        load.wait()

    sign = (1 - 2 * (lax.broadcasted_iota(jnp.int32, (1, BLOCK), 1) % 2)).astype(jnp.float32)

    last = None
    for d in range(n):
        spec = dot3(f[:, d * BLOCK : (d + 1) * BLOCK], wh[...], wl[...])
        real, imag = spec[:, :BLOCK], spec[:, BLOCK:]
        if last is None:
            fs[0, d], fs[1, d] = real, imag
        else:
            fs[0, d] = real - sign * last[1]
            fs[1, d] = imag + sign * last[0]
        last = (real, imag)

    zero = jnp.zeros((cc, BLOCK), jnp.float32)

    for c in range(chunks):
        part = pl.ds(c * cc, cc)
        for o in offsets:
            out_copy(c, o).wait_recv()
        spec = dot3(recv[c].reshape(n * 2 * cc, BLOCK), wh[...], wl[...])
        for j in range(n):
            for a in range(2):
                rows = slice((2 * j + a) * cc, (2 * j + a + 1) * cc)
                xs[a, 0, j] = spec[rows, :BLOCK]
                xs[a, 1, j] = spec[rows, BLOCK:]

        def conv_block(i):
            def step(j, carry):
                fr, fi = fs[0, i - j, part], fs[1, i - j, part]
                gr, gi = xs[0, 0, j], xs[0, 1, j]
                return (carry[0] + (fr * gr - fi * gi), carry[1] + (fr * gi + fi * gr))

            real, imag = fold(0, i + 1, step, (zero, zero))
            zs[0, i, :, :BLOCK] = real
            zs[0, i, :, BLOCK:] = imag

        def grad_block(j):
            def step(i, carry):
                fr, fi = fs[0, i - j, part], fs[1, i - j, part]
                dr, di = xs[1, 0, i], xs[1, 1, i]
                return (carry[0] + (fr * dr + fi * di), carry[1] + (fr * di - fi * dr))

            real, imag = fold(j, n, step, (zero, zero))
            zs[1, j, :, :BLOCK] = real
            zs[1, j, :, BLOCK:] = imag

        def filt_block(d):
            def step(j, carry):
                gr, gi = xs[0, 0, j], xs[0, 1, j]
                dr, di = xs[1, 0, j + d], xs[1, 1, j + d]
                return (carry[0] + (gr * dr + gi * di), carry[1] + (gr * di - gi * dr))

            real, imag = fold(0, n - d, step, (zero, zero))
            hs[0, d] = real
            hs[1, d] = imag

        each(n, conv_block)
        each(n, grad_block)
        time = dot3(zs[0:2].reshape(2 * n * cc, 2 * BLOCK), ah[...], al[...])
        for a in range(2):
            for i in range(n):
                at = (a * n + i) * cc
                ret[c, i, a] = time[at : at + cc]
        for o in offsets:
            back_copy(c, o).start()
        back[me, c] = ret[c, me]

        each(n, filt_block)
        for d in range(n):
            real, imag = hs[0, d], hs[1, d]
            if d + 1 < n:
                real, imag = real + sign * hs[1, d + 1], imag - sign * hs[0, d + 1]
            zs[2, d, :, :BLOCK] = real
            zs[2, d, :, BLOCK:] = imag
        time = dot3(zs[2].reshape(n * cc, 2 * BLOCK), ah[...], al[...])
        for d in range(n):
            fb[row, c, d] = time[d * cc : (d + 1) * cc]
        for o in range(1, nd):
            filt_copy(c, o).start()

    for c in range(chunks):
        for o in offsets:
            back_copy(c, o).wait_recv()
        for p in range(n):
            rows = pl.ds(p * ch + c * cc, cc)
            conv, grad = back[p, c, 0], back[p, c, 1]
            out_q[0, rows, :] = q[rows, :] * conv
            out_g[0, rows, :] = g[rows, :] * conv
            out_k[0, rows, :] = grad * v[rows, :]
            out_v[0, rows, :] = grad * k[rows, :]
    for c in range(chunks):
        for o in range(1, nd):
            filt_copy(c, o).wait_recv()
        for d in range(n):
            total = fb[0, c, d]
            for b in range(1, nd):
                total = total + fb[b, c, d]
            out_f[c * cc : (c + 1) * cc, d * BLOCK : (d + 1) * BLOCK] = total * scale
    for c in range(chunks):
        for o in offsets:
            out_copy(c, o).wait_send()
            back_copy(c, o).wait_send()
        for o in range(1, nd):
            filt_copy(c, o).wait_send()


def body(query, key_in, value, grad_out, filt):
    n, nd = lax.axis_size("seq"), lax.axis_size("dp")
    ch, length = filt.shape
    cc = CHUNK
    chunks = ch // cc
    scale = 1.0 / math.sqrt(nd * query.shape[0] * length)
    f32 = jnp.float32
    local = query.shape[1:]
    shape = functools.partial(jax.ShapeDtypeStruct, dtype=f32)
    dma = pltpu.SemaphoreType.DMA
    vmem = functools.partial(pltpu.VMEM, dtype=f32)
    full = tables()
    call = pl.pallas_call(
        functools.partial(kernel, n, nd, ch, cc, scale),
        out_shape=[shape(query.shape)] * 4 + [shape(filt.shape)],
        in_specs=[pl.BlockSpec(memory_space=pl.ANY)] * 9,
        out_specs=[pl.BlockSpec(memory_space=pltpu.VMEM)] * 5,
        scratch_shapes=[vmem(local)] * 4
        + [vmem(filt.shape)]
        + [pltpu.VMEM(t.shape, jnp.bfloat16) for t in full]
        + [
            vmem((n, chunks, 2, cc, BLOCK)),
            vmem((chunks, n, 2, cc, BLOCK)),
            vmem((2, n, ch, BLOCK)),
            vmem((2, 2, n, cc, BLOCK)),
            vmem((2, n, cc, BLOCK)),
            vmem((3, n, cc, 2 * BLOCK)),
            vmem((chunks, n, 2, cc, BLOCK)),
            vmem((n, chunks, 2, cc, BLOCK)),
            vmem((nd, chunks, n, cc, BLOCK)),
            dma((9,)),
            dma((chunks, n - 1)),
            dma((chunks, n - 1)),
            dma((chunks, n - 1)),
            dma((chunks, n - 1)),
            dma((chunks, nd - 1)),
            dma((chunks, nd - 1)),
        ],
        compiler_params=pltpu.CompilerParams(
            collective_id=0, has_side_effects=True, vmem_limit_bytes=24 * 1024 * 1024
        ),
    )
    return tuple(call(query, key_in, value, grad_out, filt, *(jnp.asarray(t) for t in full)))


def solution(mesh):
    spread = P("dp", None, "seq")
    return jax.shard_map(
        body,
        mesh=mesh,
        in_specs=(spread,) * 4 + (P("seq", None),),
        out_specs=(spread,) * 4 + (P("seq", None),),
        check_vma=False,
    )
```

```python
import functools
import math

import jax
import jax.numpy as jnp
import ml_dtypes
import numpy as np
from jax import lax
from jax.experimental import pallas as pl
from jax.experimental.pallas import tpu as pltpu
from jax.sharding import PartitionSpec as P

MESH = pl.DeviceIdType.MESH
BLOCK = 128
CHUNK = 8
UNROLL = 8
GRANT = 63 * 1024 * 1024


def tables():
    place = np.arange(BLOCK, dtype=np.float64)
    angle = np.pi * place[:, None] * (2.0 * place[None, :] + 1.0) / (2 * BLOCK)
    ahead = np.concatenate([np.cos(angle), -np.sin(angle)], axis=1)
    back = ahead.T / BLOCK

    def split(table):
        high = table.astype(ml_dtypes.bfloat16)
        low = (table - high.astype(np.float64)).astype(ml_dtypes.bfloat16)
        return (high, low)

    return split(ahead) + split(back)


def dot3(x, high, low):
    x_high = x.astype(jnp.bfloat16)
    x_low = (x - x_high.astype(jnp.float32)).astype(jnp.bfloat16)
    dot = functools.partial(jnp.dot, preferred_element_type=jnp.float32)
    return dot(x_high, high) + (dot(x_low, high) + dot(x_high, low))


def fold(low, high, step, carry):
    if isinstance(low, int) and isinstance(high, int):
        for at in range(low, high):
            carry = step(at, carry)
        return carry
    return lax.fori_loop(low, high, step, carry)


def each(count, step):
    if count <= UNROLL:
        for at in range(count):
            step(at)
    else:

        @pl.loop(0, count)
        def _(at):
            step(at)


def kernel(
    n, nd, ch, cc, scale,
    q_hbm, k_hbm, v_hbm, g_hbm, f_hbm, wh_hbm, wl_hbm, ah_hbm, al_hbm,
    oq_hbm, og_hbm, ok_hbm, ov_hbm, of_hbm,
    q, k, v, g, f, wh, wl, ah, al,
    out_q, out_g, out_k, out_v, out_f,
    send, recv, fs, xs, hs, zs, ret, back, fb,
    load_sem, save_sem, s_sem, r_sem, bs_sem, br_sem, fs_sem, fr_sem,
):
    me = lax.axis_index("seq")
    row = lax.axis_index("dp")
    chunks = ch // cc
    offsets = sorted(range(1, n), key=lambda o: -min(o, n - o))

    loads = [
        pltpu.make_async_copy(src, dst, load_sem.at[at])
        for at, (src, dst) in enumerate(
            [
                (k_hbm.at[0], k), (v_hbm.at[0], v), (q_hbm.at[0], q), (g_hbm.at[0], g),
                (f_hbm, f), (wh_hbm, wh), (wl_hbm, wl), (ah_hbm, ah), (al_hbm, al),
            ]
        )
    ]
    for load in loads:
        load.start()

    barrier = pltpu.get_barrier_semaphore()
    for o in range(1, n):
        pl.semaphore_signal(
            barrier, inc=1, device_id={"seq": lax.rem(me + o, n)}, device_id_type=MESH
        )
    for o in range(1, nd):
        pl.semaphore_signal(
            barrier, inc=1, device_id={"dp": lax.rem(row + o, nd)}, device_id_type=MESH
        )

    for load in loads[:4]:
        load.wait()

    def stage(c):
        for p in range(n):
            rows = pl.ds(p * ch + c * cc, cc)
            send[p, c, 0] = k[rows, :] * v[rows, :]
            send[p, c, 1] = g[rows, :] * q[rows, :]
        recv[c, me] = send[me, c]

    def out_copy(c, o):
        to = lax.rem(me + o, n)
        return pltpu.make_async_remote_copy(
            src_ref=send.at[to, c],
            dst_ref=recv.at[c, me],
            send_sem=s_sem.at[c, o - 1],
            recv_sem=r_sem.at[c, o - 1],
            device_id={"seq": to},
            device_id_type=MESH,
        )

    def back_copy(c, o):
        to = lax.rem(me + o, n)
        return pltpu.make_async_remote_copy(
            src_ref=ret.at[c, to],
            dst_ref=back.at[me, c],
            send_sem=bs_sem.at[c, o - 1],
            recv_sem=br_sem.at[c, o - 1],
            device_id={"seq": to},
            device_id_type=MESH,
        )

    def filt_copy(c, o):
        return pltpu.make_async_remote_copy(
            src_ref=fb.at[row, c],
            dst_ref=fb.at[row, c],
            send_sem=fs_sem.at[c, o - 1],
            recv_sem=fr_sem.at[c, o - 1],
            device_id={"dp": lax.rem(row + o, nd)},
            device_id_type=MESH,
        )

    for c in range(chunks):
        stage(c)
        if c == 0:
            pl.semaphore_wait(barrier, n - 1 + nd - 1)
        for o in offsets:
            out_copy(c, o).start()

    for load in loads[4:]:
        load.wait()

    sign = (1 - 2 * (lax.broadcasted_iota(jnp.int32, (1, BLOCK), 1) % 2)).astype(jnp.float32)

    last = None
    for d in range(n):
        spec = dot3(f[:, d * BLOCK : (d + 1) * BLOCK], wh[...], wl[...])
        real, imag = spec[:, :BLOCK], spec[:, BLOCK:]
        if last is None:
            fs[0, d], fs[1, d] = real, imag
        else:
            fs[0, d] = real - sign * last[1]
            fs[1, d] = imag + sign * last[0]
        last = (real, imag)

    zero = jnp.zeros((cc, BLOCK), jnp.float32)

    for c in range(chunks):
        part = pl.ds(c * cc, cc)
        for o in offsets:
            out_copy(c, o).wait_recv()
        spec = dot3(recv[c].reshape(n * 2 * cc, BLOCK), wh[...], wl[...])
        for j in range(n):
            for a in range(2):
                rows = slice((2 * j + a) * cc, (2 * j + a + 1) * cc)
                xs[a, 0, j] = spec[rows, :BLOCK]
                xs[a, 1, j] = spec[rows, BLOCK:]

        def conv_block(i):
            def step(j, carry):
                fr, fi = fs[0, i - j, part], fs[1, i - j, part]
                gr, gi = xs[0, 0, j], xs[0, 1, j]
                return (carry[0] + (fr * gr - fi * gi), carry[1] + (fr * gi + fi * gr))

            real, imag = fold(0, i + 1, step, (zero, zero))
            zs[0, i, :, :BLOCK] = real
            zs[0, i, :, BLOCK:] = imag

        def grad_block(j):
            def step(i, carry):
                fr, fi = fs[0, i - j, part], fs[1, i - j, part]
                dr, di = xs[1, 0, i], xs[1, 1, i]
                return (carry[0] + (fr * dr + fi * di), carry[1] + (fr * di - fi * dr))

            real, imag = fold(j, n, step, (zero, zero))
            zs[1, j, :, :BLOCK] = real
            zs[1, j, :, BLOCK:] = imag

        def filt_block(d):
            def step(j, carry):
                gr, gi = xs[0, 0, j], xs[0, 1, j]
                dr, di = xs[1, 0, j + d], xs[1, 1, j + d]
                return (carry[0] + (gr * dr + gi * di), carry[1] + (gr * di - gi * dr))

            real, imag = fold(0, n - d, step, (zero, zero))
            hs[0, d] = real
            hs[1, d] = imag

        each(n, conv_block)
        each(n, grad_block)
        time = dot3(zs[0:2].reshape(2 * n * cc, 2 * BLOCK), ah[...], al[...])
        for a in range(2):
            for i in range(n):
                at = (a * n + i) * cc
                ret[c, i, a] = time[at : at + cc]
        for o in offsets:
            back_copy(c, o).start()
        back[me, c] = ret[c, me]

        each(n, filt_block)
        for d in range(n):
            real, imag = hs[0, d], hs[1, d]
            if d + 1 < n:
                real, imag = real + sign * hs[1, d + 1], imag - sign * hs[0, d + 1]
            zs[2, d, :, :BLOCK] = real
            zs[2, d, :, BLOCK:] = imag
        time = dot3(zs[2].reshape(n * cc, 2 * BLOCK), ah[...], al[...])
        for d in range(n):
            fb[row, c, d] = time[d * cc : (d + 1) * cc]
        for o in range(1, nd):
            filt_copy(c, o).start()

    for c in range(chunks):
        for o in offsets:
            back_copy(c, o).wait_recv()
        for p in range(n):
            rows = pl.ds(p * ch + c * cc, cc)
            conv, grad = back[p, c, 0], back[p, c, 1]
            out_q[rows, :] = q[rows, :] * conv
            out_g[rows, :] = g[rows, :] * conv
            out_k[rows, :] = grad * v[rows, :]
            out_v[rows, :] = grad * k[rows, :]
    saves = [
        pltpu.make_async_copy(src, dst, save_sem.at[at])
        for at, (src, dst) in enumerate(
            [
                (out_q, oq_hbm.at[0]), (out_g, og_hbm.at[0]), (out_k, ok_hbm.at[0]),
                (out_v, ov_hbm.at[0]), (out_f, of_hbm),
            ]
        )
    ]
    for save in saves[:4]:
        save.start()
    for c in range(chunks):
        for o in range(1, nd):
            filt_copy(c, o).wait_recv()
        for d in range(n):
            total = fb[0, c, d]
            for b in range(1, nd):
                total = total + fb[b, c, d]
            out_f[c * cc : (c + 1) * cc, d * BLOCK : (d + 1) * BLOCK] = total * scale
    saves[4].start()
    for c in range(chunks):
        for o in offsets:
            out_copy(c, o).wait_send()
            back_copy(c, o).wait_send()
        for o in range(1, nd):
            filt_copy(c, o).wait_send()
    for save in saves:
        save.wait()


def writer(*refs):
    source, target, held = refs[:5], refs[5:10], refs[10:15]
    load_sem, save_sem = refs[15:]
    loads = [pltpu.make_async_copy(source[at], held[at], load_sem.at[at]) for at in range(5)]
    saves = [pltpu.make_async_copy(held[at], target[at], save_sem.at[at]) for at in range(5)]
    for load in loads:
        load.start()
    for load, save in zip(loads, saves):
        load.wait()
        save.start()
    for save in saves:
        save.wait()


def body(query, key_in, value, grad_out, filt):
    n, nd = lax.axis_size("seq"), lax.axis_size("dp")
    ch, length = filt.shape
    cc = CHUNK
    chunks = ch // cc
    scale = 1.0 / math.sqrt(nd * query.shape[0] * length)
    f32 = jnp.float32
    local = query.shape[1:]
    shape = functools.partial(jax.ShapeDtypeStruct, dtype=f32)
    dma = pltpu.SemaphoreType.DMA
    vmem = functools.partial(pltpu.VMEM, dtype=f32)
    full = tables()
    call = pl.pallas_call(
        functools.partial(kernel, n, nd, ch, cc, scale),
        out_shape=[shape(query.shape)] * 4 + [shape(filt.shape)],
        in_specs=[pl.BlockSpec(memory_space=pltpu.HBM)] * 9,
        out_specs=[pl.BlockSpec(memory_space=pltpu.HBM)] * 5,
        scratch_shapes=[vmem(local)] * 4
        + [vmem(filt.shape)]
        + [pltpu.VMEM(t.shape, jnp.bfloat16) for t in full]
        + [vmem(local)] * 4
        + [vmem(filt.shape)]
        + [
            vmem((n, chunks, 2, cc, BLOCK)),
            vmem((chunks, n, 2, cc, BLOCK)),
            vmem((2, n, ch, BLOCK)),
            vmem((2, 2, n, cc, BLOCK)),
            vmem((2, n, cc, BLOCK)),
            vmem((3, n, cc, 2 * BLOCK)),
            vmem((chunks, n, 2, cc, BLOCK)),
            vmem((n, chunks, 2, cc, BLOCK)),
            vmem((nd, chunks, n, cc, BLOCK)),
            dma((9,)),
            dma((5,)),
            dma((chunks, n - 1)),
            dma((chunks, n - 1)),
            dma((chunks, n - 1)),
            dma((chunks, n - 1)),
            dma((chunks, nd - 1)),
            dma((chunks, nd - 1)),
        ],
        compiler_params=pltpu.CompilerParams(
            collective_id=0, has_side_effects=True, vmem_limit_bytes=GRANT
        ),
    )
    done = call(query, key_in, value, grad_out, filt, *(jnp.asarray(t) for t in full))
    store = pl.pallas_call(
        writer,
        out_shape=[shape(query.shape)] * 4 + [shape(filt.shape)],
        in_specs=[pl.BlockSpec(memory_space=pltpu.HBM)] * 5,
        out_specs=[pl.BlockSpec(memory_space=pltpu.HBM)] * 5,
        scratch_shapes=[vmem(query.shape)] * 4 + [vmem(filt.shape), dma((5,)), dma((5,))],
        compiler_params=pltpu.CompilerParams(vmem_limit_bytes=GRANT),
    )
    return tuple(store(*done))


def solution(mesh):
    spread = P("dp", None, "seq")
    return jax.shard_map(
        body,
        mesh=mesh,
        in_specs=(spread,) * 4 + (P("seq", None),),
        out_specs=(spread,) * 4 + (P("seq", None),),
        check_vma=False,
    )
```

```python
import functools
import math

import jax
import jax.numpy as jnp
import ml_dtypes
import numpy as np
from jax import lax
from jax.experimental import pallas as pl
from jax.experimental.pallas import tpu as pltpu
from jax.sharding import PartitionSpec as P

MESH = pl.DeviceIdType.MESH
BLOCK = 128
CHUNK = 8
UNROLL = 8
GRANT = 24 * 1024 * 1024


def tables():
    place = np.arange(BLOCK, dtype=np.float64)
    angle = np.pi * place[:, None] * (2.0 * place[None, :] + 1.0) / (2 * BLOCK)
    ahead = np.concatenate([np.cos(angle), -np.sin(angle)], axis=1)
    back = ahead.T / BLOCK

    def split(table):
        high = table.astype(ml_dtypes.bfloat16)
        low = (table - high.astype(np.float64)).astype(ml_dtypes.bfloat16)
        return (high, low)

    return split(ahead) + split(back)


def dot3(x, high, low):
    x_high = x.astype(jnp.bfloat16)
    x_low = (x - x_high.astype(jnp.float32)).astype(jnp.bfloat16)
    dot = functools.partial(jnp.dot, preferred_element_type=jnp.float32)
    return dot(x_high, high) + (dot(x_low, high) + dot(x_high, low))


def fold(low, high, step, carry):
    if isinstance(low, int) and isinstance(high, int):
        for at in range(low, high):
            carry = step(at, carry)
        return carry
    return lax.fori_loop(low, high, step, carry)


def each(count, step):
    if count <= UNROLL:
        for at in range(count):
            step(at)
    else:

        @pl.loop(0, count)
        def _(at):
            step(at)


def kernel(
    n, nd, ch, cc, scale,
    q_hbm, k_hbm, v_hbm, g_hbm, f_hbm, wh_hbm, wl_hbm, ah_hbm, al_hbm,
    out_q, out_g, out_k, out_v, out_f,
    q, k, v, g, f, wh, wl, ah, al,
    send, recv, fs, xs, hs, zs, ret, back, fb,
    load_sem, s_sem, r_sem, bs_sem, br_sem, fs_sem, fr_sem,
):
    me = lax.axis_index("seq")
    row = lax.axis_index("dp")
    chunks = ch // cc
    offsets = sorted(range(1, n), key=lambda o: -min(o, n - o))

    loads = [
        pltpu.make_async_copy(src, dst, load_sem.at[at])
        for at, (src, dst) in enumerate(
            [
                (k_hbm.at[0], k), (v_hbm.at[0], v), (q_hbm.at[0], q), (g_hbm.at[0], g),
                (f_hbm, f), (wh_hbm, wh), (wl_hbm, wl), (ah_hbm, ah), (al_hbm, al),
            ]
        )
    ]
    for load in loads:
        load.start()

    barrier = pltpu.get_barrier_semaphore()
    for o in range(1, n):
        pl.semaphore_signal(
            barrier, inc=1, device_id={"seq": lax.rem(me + o, n)}, device_id_type=MESH
        )
    for o in range(1, nd):
        pl.semaphore_signal(
            barrier, inc=1, device_id={"dp": lax.rem(row + o, nd)}, device_id_type=MESH
        )

    for load in loads[:4]:
        load.wait()

    def stage(c):
        for p in range(n):
            rows = pl.ds(p * ch + c * cc, cc)
            send[p, c, 0] = k[rows, :] * v[rows, :]
            send[p, c, 1] = g[rows, :] * q[rows, :]
        recv[c, me] = send[me, c]

    def out_copy(c, o):
        to = lax.rem(me + o, n)
        return pltpu.make_async_remote_copy(
            src_ref=send.at[to, c],
            dst_ref=recv.at[c, me],
            send_sem=s_sem.at[c, o - 1],
            recv_sem=r_sem.at[c, o - 1],
            device_id={"seq": to},
            device_id_type=MESH,
        )

    def back_copy(c, o):
        to = lax.rem(me + o, n)
        return pltpu.make_async_remote_copy(
            src_ref=ret.at[c, to],
            dst_ref=back.at[me, c],
            send_sem=bs_sem.at[c, o - 1],
            recv_sem=br_sem.at[c, o - 1],
            device_id={"seq": to},
            device_id_type=MESH,
        )

    def filt_copy(c, o):
        return pltpu.make_async_remote_copy(
            src_ref=fb.at[row, c],
            dst_ref=fb.at[row, c],
            send_sem=fs_sem.at[c, o - 1],
            recv_sem=fr_sem.at[c, o - 1],
            device_id={"dp": lax.rem(row + o, nd)},
            device_id_type=MESH,
        )

    for c in range(chunks):
        stage(c)
        if c == 0:
            pl.semaphore_wait(barrier, n - 1 + nd - 1)
        for o in offsets:
            out_copy(c, o).start()

    for load in loads[4:]:
        load.wait()

    sign = (1 - 2 * (lax.broadcasted_iota(jnp.int32, (1, BLOCK), 1) % 2)).astype(jnp.float32)

    last = None
    for d in range(n):
        spec = dot3(f[:, d * BLOCK : (d + 1) * BLOCK], wh[...], wl[...])
        real, imag = spec[:, :BLOCK], spec[:, BLOCK:]
        if last is None:
            fs[0, d], fs[1, d] = real, imag
        else:
            fs[0, d] = real - sign * last[1]
            fs[1, d] = imag + sign * last[0]
        last = (real, imag)

    zero = jnp.zeros((cc, BLOCK), jnp.float32)

    for c in range(chunks):
        part = pl.ds(c * cc, cc)
        for o in offsets:
            out_copy(c, o).wait_recv()
        spec = dot3(recv[c].reshape(n * 2 * cc, BLOCK), wh[...], wl[...])
        for j in range(n):
            for a in range(2):
                rows = slice((2 * j + a) * cc, (2 * j + a + 1) * cc)
                xs[a, 0, j] = spec[rows, :BLOCK]
                xs[a, 1, j] = spec[rows, BLOCK:]

        def conv_block(i):
            def step(j, carry):
                fr, fi = fs[0, i - j, part], fs[1, i - j, part]
                gr, gi = xs[0, 0, j], xs[0, 1, j]
                return (carry[0] + (fr * gr - fi * gi), carry[1] + (fr * gi + fi * gr))

            real, imag = fold(0, i + 1, step, (zero, zero))
            zs[0, i, :, :BLOCK] = real
            zs[0, i, :, BLOCK:] = imag

        def grad_block(j):
            def step(i, carry):
                fr, fi = fs[0, i - j, part], fs[1, i - j, part]
                dr, di = xs[1, 0, i], xs[1, 1, i]
                return (carry[0] + (fr * dr + fi * di), carry[1] + (fr * di - fi * dr))

            real, imag = fold(j, n, step, (zero, zero))
            zs[1, j, :, :BLOCK] = real
            zs[1, j, :, BLOCK:] = imag

        def filt_block(d):
            def step(j, carry):
                gr, gi = xs[0, 0, j], xs[0, 1, j]
                dr, di = xs[1, 0, j + d], xs[1, 1, j + d]
                return (carry[0] + (gr * dr + gi * di), carry[1] + (gr * di - gi * dr))

            real, imag = fold(0, n - d, step, (zero, zero))
            hs[0, d] = real
            hs[1, d] = imag

        each(n, conv_block)
        each(n, grad_block)
        time = dot3(zs[0:2].reshape(2 * n * cc, 2 * BLOCK), ah[...], al[...])
        for a in range(2):
            for i in range(n):
                at = (a * n + i) * cc
                ret[c, i, a] = time[at : at + cc]
        for o in offsets:
            back_copy(c, o).start()
        back[me, c] = ret[c, me]

        each(n, filt_block)
        for d in range(n):
            real, imag = hs[0, d], hs[1, d]
            if d + 1 < n:
                real, imag = real + sign * hs[1, d + 1], imag - sign * hs[0, d + 1]
            zs[2, d, :, :BLOCK] = real
            zs[2, d, :, BLOCK:] = imag
        time = dot3(zs[2].reshape(n * cc, 2 * BLOCK), ah[...], al[...])
        for d in range(n):
            fb[row, c, d] = time[d * cc : (d + 1) * cc]
        for o in range(1, nd):
            filt_copy(c, o).start()

    for c in range(chunks):
        for o in offsets:
            back_copy(c, o).wait_recv()
        for p in range(n):
            rows = pl.ds(p * ch + c * cc, cc)
            conv, grad = back[p, c, 0], back[p, c, 1]
            out_q[0, rows, :] = q[rows, :] * conv
            out_g[0, rows, :] = g[rows, :] * conv
            out_k[0, rows, :] = grad * v[rows, :]
            out_v[0, rows, :] = grad * k[rows, :]
    for c in range(chunks):
        for o in range(1, nd):
            filt_copy(c, o).wait_recv()
        for d in range(n):
            total = fb[0, c, d]
            for b in range(1, nd):
                total = total + fb[b, c, d]
            out_f[c * cc : (c + 1) * cc, d * BLOCK : (d + 1) * BLOCK] = total * scale
    for c in range(chunks):
        for o in offsets:
            out_copy(c, o).wait_send()
            back_copy(c, o).wait_send()
        for o in range(1, nd):
            filt_copy(c, o).wait_send()


def writer(*refs):
    sem = refs[10]
    saves = [pltpu.make_async_copy(refs[at], refs[5 + at], sem.at[at]) for at in range(5)]
    for save in saves:
        save.start()
    for save in saves:
        save.wait()


def body(query, key_in, value, grad_out, filt):
    n, nd = lax.axis_size("seq"), lax.axis_size("dp")
    ch, length = filt.shape
    cc = CHUNK
    chunks = ch // cc
    scale = 1.0 / math.sqrt(nd * query.shape[0] * length)
    f32 = jnp.float32
    local = query.shape[1:]
    shape = functools.partial(jax.ShapeDtypeStruct, dtype=f32)
    dma = pltpu.SemaphoreType.DMA
    vmem = functools.partial(pltpu.VMEM, dtype=f32)
    full = tables()
    call = pl.pallas_call(
        functools.partial(kernel, n, nd, ch, cc, scale),
        out_shape=[shape(query.shape)] * 4 + [shape(filt.shape)],
        in_specs=[pl.BlockSpec(memory_space=pltpu.HBM)] * 9,
        out_specs=[pl.BlockSpec(memory_space=pltpu.VMEM)] * 5,
        scratch_shapes=[vmem(local)] * 4
        + [vmem(filt.shape)]
        + [pltpu.VMEM(t.shape, jnp.bfloat16) for t in full]
        + [
            vmem((n, chunks, 2, cc, BLOCK)),
            vmem((chunks, n, 2, cc, BLOCK)),
            vmem((2, n, ch, BLOCK)),
            vmem((2, 2, n, cc, BLOCK)),
            vmem((2, n, cc, BLOCK)),
            vmem((3, n, cc, 2 * BLOCK)),
            vmem((chunks, n, 2, cc, BLOCK)),
            vmem((n, chunks, 2, cc, BLOCK)),
            vmem((nd, chunks, n, cc, BLOCK)),
            dma((9,)),
            dma((chunks, n - 1)),
            dma((chunks, n - 1)),
            dma((chunks, n - 1)),
            dma((chunks, n - 1)),
            dma((chunks, nd - 1)),
            dma((chunks, nd - 1)),
        ],
        compiler_params=pltpu.CompilerParams(
            collective_id=0, has_side_effects=True, vmem_limit_bytes=GRANT
        ),
    )
    operands = [query, key_in, value, grad_out, filt] + [jnp.asarray(t) for t in full]
    done = call(*(pltpu.with_memory_space_constraint(x, pltpu.HBM) for x in operands))
    store = pl.pallas_call(
        writer,
        out_shape=[shape(query.shape)] * 4 + [shape(filt.shape)],
        in_specs=[pl.BlockSpec(memory_space=pltpu.VMEM)] * 5,
        out_specs=[pl.BlockSpec(memory_space=pltpu.HBM)] * 5,
        scratch_shapes=[dma((5,))],
        compiler_params=pltpu.CompilerParams(vmem_limit_bytes=GRANT),
    )
    return tuple(store(*done))


def solution(mesh):
    spread = P("dp", None, "seq")
    return jax.shard_map(
        body,
        mesh=mesh,
        in_specs=(spread,) * 4 + (P("seq", None),),
        out_specs=(spread,) * 4 + (P("seq", None),),
        check_vma=False,
    )
```

```python
import functools
import math

import jax
import jax.numpy as jnp
import ml_dtypes
import numpy as np
from jax import lax
from jax.experimental import pallas as pl
from jax.experimental.pallas import tpu as pltpu
from jax.sharding import PartitionSpec as P

MESH = pl.DeviceIdType.MESH
BLOCK = 128
CHUNK = 8
UNROLL = 8
GRANT = 24 * 1024 * 1024


def tables():
    place = np.arange(BLOCK, dtype=np.float64)
    angle = np.pi * place[:, None] * (2.0 * place[None, :] + 1.0) / (2 * BLOCK)
    ahead = np.concatenate([np.cos(angle), -np.sin(angle)], axis=1)
    back = ahead.T / BLOCK

    def split(table):
        high = table.astype(ml_dtypes.bfloat16)
        low = (table - high.astype(np.float64)).astype(ml_dtypes.bfloat16)
        return (high, low)

    return split(ahead) + split(back)


def dot3(x, high, low):
    x_high = x.astype(jnp.bfloat16)
    x_low = (x - x_high.astype(jnp.float32)).astype(jnp.bfloat16)
    dot = functools.partial(jnp.dot, preferred_element_type=jnp.float32)
    return dot(x_high, high) + (dot(x_low, high) + dot(x_high, low))


def fold(low, high, step, carry):
    if isinstance(low, int) and isinstance(high, int):
        for at in range(low, high):
            carry = step(at, carry)
        return carry
    return lax.fori_loop(low, high, step, carry)


def each(count, step):
    if count <= UNROLL:
        for at in range(count):
            step(at)
    else:

        @pl.loop(0, count)
        def _(at):
            step(at)


def kernel(
    n, nd, ch, cc, scale,
    q_hbm, k_hbm, v_hbm, g_hbm, f_hbm, wh_hbm, wl_hbm, ah_hbm, al_hbm,
    out_q, out_g, out_k, out_v, out_f,
    q, k, v, g, f, wh, wl, ah, al,
    send, recv, fs, xs, hs, zs, ret, back, fb,
    load_sem, s_sem, r_sem, bs_sem, br_sem, fs_sem, fr_sem,
):
    me = lax.axis_index("seq")
    row = lax.axis_index("dp")
    chunks = ch // cc
    half = n // 2
    offsets = range(1, n)
    side = me // half * half

    def partner(o):
        if o <= half:
            return lax.rem(side + half, n) + lax.rem(me - side + o - 1, half)
        return side + lax.rem(me - side + o - half, half)


    loads = [
        pltpu.make_async_copy(src, dst, load_sem.at[at])
        for at, (src, dst) in enumerate(
            [
                (k_hbm.at[0], k), (v_hbm.at[0], v), (q_hbm.at[0], q), (g_hbm.at[0], g),
                (f_hbm, f), (wh_hbm, wh), (wl_hbm, wl), (ah_hbm, ah), (al_hbm, al),
            ]
        )
    ]
    for load in loads:
        load.start()

    barrier = pltpu.get_barrier_semaphore()
    for o in range(1, n):
        pl.semaphore_signal(
            barrier, inc=1, device_id={"seq": lax.rem(me + o, n)}, device_id_type=MESH
        )
    for o in range(1, nd):
        pl.semaphore_signal(
            barrier, inc=1, device_id={"dp": lax.rem(row + o, nd)}, device_id_type=MESH
        )

    for load in loads[:4]:
        load.wait()

    def stage(c):
        for p in range(n):
            rows = pl.ds(p * ch + c * cc, cc)
            send[p, c, 0] = k[rows, :] * v[rows, :]
            send[p, c, 1] = g[rows, :] * q[rows, :]
        recv[c, me] = send[me, c]

    def out_copy(c, o):
        to = partner(o)
        return pltpu.make_async_remote_copy(
            src_ref=send.at[to, c],
            dst_ref=recv.at[c, me],
            send_sem=s_sem.at[c, o - 1],
            recv_sem=r_sem.at[c, o - 1],
            device_id={"seq": to},
            device_id_type=MESH,
        )

    def back_copy(c, o):
        to = partner(o)
        return pltpu.make_async_remote_copy(
            src_ref=ret.at[c, to],
            dst_ref=back.at[me, c],
            send_sem=bs_sem.at[c, o - 1],
            recv_sem=br_sem.at[c, o - 1],
            device_id={"seq": to},
            device_id_type=MESH,
        )

    def filt_copy(c, o):
        return pltpu.make_async_remote_copy(
            src_ref=fb.at[row, c],
            dst_ref=fb.at[row, c],
            send_sem=fs_sem.at[c, o - 1],
            recv_sem=fr_sem.at[c, o - 1],
            device_id={"dp": lax.rem(row + o, nd)},
            device_id_type=MESH,
        )

    for c in range(chunks):
        stage(c)
        if c == 0:
            pl.semaphore_wait(barrier, n - 1 + nd - 1)
        for o in offsets:
            out_copy(c, o).start()

    for load in loads[4:]:
        load.wait()

    sign = (1 - 2 * (lax.broadcasted_iota(jnp.int32, (1, BLOCK), 1) % 2)).astype(jnp.float32)

    last = None
    for d in range(n):
        spec = dot3(f[:, d * BLOCK : (d + 1) * BLOCK], wh[...], wl[...])
        real, imag = spec[:, :BLOCK], spec[:, BLOCK:]
        if last is None:
            fs[0, d], fs[1, d] = real, imag
        else:
            fs[0, d] = real - sign * last[1]
            fs[1, d] = imag + sign * last[0]
        last = (real, imag)

    zero = jnp.zeros((cc, BLOCK), jnp.float32)

    for c in range(chunks):
        part = pl.ds(c * cc, cc)
        for o in offsets:
            out_copy(c, o).wait_recv()
        spec = dot3(recv[c].reshape(n * 2 * cc, BLOCK), wh[...], wl[...])
        for j in range(n):
            for a in range(2):
                rows = slice((2 * j + a) * cc, (2 * j + a + 1) * cc)
                xs[a, 0, j] = spec[rows, :BLOCK]
                xs[a, 1, j] = spec[rows, BLOCK:]

        def conv_block(i):
            def step(j, carry):
                fr, fi = fs[0, i - j, part], fs[1, i - j, part]
                gr, gi = xs[0, 0, j], xs[0, 1, j]
                return (carry[0] + (fr * gr - fi * gi), carry[1] + (fr * gi + fi * gr))

            real, imag = fold(0, i + 1, step, (zero, zero))
            zs[0, i, :, :BLOCK] = real
            zs[0, i, :, BLOCK:] = imag

        def grad_block(j):
            def step(i, carry):
                fr, fi = fs[0, i - j, part], fs[1, i - j, part]
                dr, di = xs[1, 0, i], xs[1, 1, i]
                return (carry[0] + (fr * dr + fi * di), carry[1] + (fr * di - fi * dr))

            real, imag = fold(j, n, step, (zero, zero))
            zs[1, j, :, :BLOCK] = real
            zs[1, j, :, BLOCK:] = imag

        def filt_block(d):
            def step(j, carry):
                gr, gi = xs[0, 0, j], xs[0, 1, j]
                dr, di = xs[1, 0, j + d], xs[1, 1, j + d]
                return (carry[0] + (gr * dr + gi * di), carry[1] + (gr * di - gi * dr))

            real, imag = fold(0, n - d, step, (zero, zero))
            hs[0, d] = real
            hs[1, d] = imag

        each(n, conv_block)
        each(n, grad_block)
        time = dot3(zs[0:2].reshape(2 * n * cc, 2 * BLOCK), ah[...], al[...])
        for a in range(2):
            for i in range(n):
                at = (a * n + i) * cc
                ret[c, i, a] = time[at : at + cc]
        for o in offsets:
            back_copy(c, o).start()
        back[me, c] = ret[c, me]

        each(n, filt_block)
        for d in range(n):
            real, imag = hs[0, d], hs[1, d]
            if d + 1 < n:
                real, imag = real + sign * hs[1, d + 1], imag - sign * hs[0, d + 1]
            zs[2, d, :, :BLOCK] = real
            zs[2, d, :, BLOCK:] = imag
        time = dot3(zs[2].reshape(n * cc, 2 * BLOCK), ah[...], al[...])
        for d in range(n):
            fb[row, c, d] = time[d * cc : (d + 1) * cc]
        for o in range(1, nd):
            filt_copy(c, o).start()

    for c in range(chunks):
        for o in offsets:
            back_copy(c, o).wait_recv()
        for p in range(n):
            rows = pl.ds(p * ch + c * cc, cc)
            conv, grad = back[p, c, 0], back[p, c, 1]
            out_q[0, rows, :] = q[rows, :] * conv
            out_g[0, rows, :] = g[rows, :] * conv
            out_k[0, rows, :] = grad * v[rows, :]
            out_v[0, rows, :] = grad * k[rows, :]
    for c in range(chunks):
        for o in range(1, nd):
            filt_copy(c, o).wait_recv()
        for d in range(n):
            total = fb[0, c, d]
            for b in range(1, nd):
                total = total + fb[b, c, d]
            out_f[c * cc : (c + 1) * cc, d * BLOCK : (d + 1) * BLOCK] = total * scale
    for c in range(chunks):
        for o in offsets:
            out_copy(c, o).wait_send()
            back_copy(c, o).wait_send()
        for o in range(1, nd):
            filt_copy(c, o).wait_send()


def writer(*refs):
    sem = refs[10]
    saves = [pltpu.make_async_copy(refs[at], refs[5 + at], sem.at[at]) for at in range(5)]
    for save in saves:
        save.start()
    for save in saves:
        save.wait()


def body(query, key_in, value, grad_out, filt):
    n, nd = lax.axis_size("seq"), lax.axis_size("dp")
    ch, length = filt.shape
    cc = CHUNK
    chunks = ch // cc
    scale = 1.0 / math.sqrt(nd * query.shape[0] * length)
    f32 = jnp.float32
    local = query.shape[1:]
    shape = functools.partial(jax.ShapeDtypeStruct, dtype=f32)
    dma = pltpu.SemaphoreType.DMA
    vmem = functools.partial(pltpu.VMEM, dtype=f32)
    full = tables()
    call = pl.pallas_call(
        functools.partial(kernel, n, nd, ch, cc, scale),
        out_shape=[shape(query.shape)] * 4 + [shape(filt.shape)],
        in_specs=[pl.BlockSpec(memory_space=pltpu.HBM)] * 9,
        out_specs=[pl.BlockSpec(memory_space=pltpu.VMEM)] * 5,
        scratch_shapes=[vmem(local)] * 4
        + [vmem(filt.shape)]
        + [pltpu.VMEM(t.shape, jnp.bfloat16) for t in full]
        + [
            vmem((n, chunks, 2, cc, BLOCK)),
            vmem((chunks, n, 2, cc, BLOCK)),
            vmem((2, n, ch, BLOCK)),
            vmem((2, 2, n, cc, BLOCK)),
            vmem((2, n, cc, BLOCK)),
            vmem((3, n, cc, 2 * BLOCK)),
            vmem((chunks, n, 2, cc, BLOCK)),
            vmem((n, chunks, 2, cc, BLOCK)),
            vmem((nd, chunks, n, cc, BLOCK)),
            dma((9,)),
            dma((chunks, n - 1)),
            dma((chunks, n - 1)),
            dma((chunks, n - 1)),
            dma((chunks, n - 1)),
            dma((chunks, nd - 1)),
            dma((chunks, nd - 1)),
        ],
        compiler_params=pltpu.CompilerParams(
            collective_id=0, has_side_effects=True, vmem_limit_bytes=GRANT
        ),
    )
    operands = [query, key_in, value, grad_out, filt] + [jnp.asarray(t) for t in full]
    done = call(*(pltpu.with_memory_space_constraint(x, pltpu.HBM) for x in operands))
    store = pl.pallas_call(
        writer,
        out_shape=[shape(query.shape)] * 4 + [shape(filt.shape)],
        in_specs=[pl.BlockSpec(memory_space=pltpu.VMEM)] * 5,
        out_specs=[pl.BlockSpec(memory_space=pltpu.HBM)] * 5,
        scratch_shapes=[dma((5,))],
        compiler_params=pltpu.CompilerParams(vmem_limit_bytes=GRANT),
    )
    return tuple(store(*done))


def solution(mesh):
    spread = P("dp", None, "seq")
    return jax.shard_map(
        body,
        mesh=mesh,
        in_specs=(spread,) * 4 + (P("seq", None),),
        out_specs=(spread,) * 4 + (P("seq", None),),
        check_vma=False,
    )
```
